512 devices in a mesh: ex: 32 (over y, x_hi, core), layer: 16 (over x_lo, z).
Axes of the slice: x: 4 (x_hi: 2, x_lo: 2; x = x_hi * 2 + x_lo), y: 8, z: 8, core: 2. Of those that a mesh axis runs over, the one named last changes fastest.
Arguments:
- queries: bfloat16 [16, 1024, 4096], P('layer', 'ex'), may hold values from -6 to 6
- train_grads: bfloat16 [16, 16384, 4096], P('layer', 'ex'), may hold values from -0.09375 to 0.09375
- basis_in: float32 [16, 64, 64], P('layer'), may hold values from -0.75 to 0.75
- basis_out: float32 [16, 64, 64], P('layer'), may hold values from -0.75 to 0.75
- inverse_eigen: float32 [16, 64, 64], P('layer'), may hold values from 0.05 to 1
Outputs:
- scores: float32 [1024, 16384], P('layer', 'ex')
The draws below stay inside these ranges and needn't reach their ends.
All inputs are finite; a program needn't handle non-finite values.
Results may differ from the reference program's by a relative error of at most 0.0029.
Values may be sent and summed in bfloat16 or wider, within the bound.
A program may use at most 64 MiB of HBM per device.

```python
import math
import jax
import jax.numpy as jnp
from jax import lax

IN_DIM = 64
OUT_DIM = 64
GRAD = 4096
LAYERS = 16
NQ = 1024
NTRAIN = 16384


def levels(rng, dims, cuts, smallest, top_value):
    gain, own = 1.0, jax.random.fold_in(rng, 6)
    for dim, blocks in cuts:
        steps = jnp.exp(jax.random.uniform(jax.random.fold_in(own, dim), (blocks,), jnp.float32, smallest / len(cuts), top_value / len(cuts)))
        gain = gain * jnp.repeat(steps, dims[dim] // blocks).reshape([-1 if axis == dim else 1 for axis in range(len(dims))])
    return gain


def normal_values(own_key, shape, width, most, cuts=(), dtype=jnp.bfloat16):
    factor_of = levels(own_key, shape, cuts, -0.22, 0.18) if cuts else 1.0
    result = jax.random.normal(own_key, shape, jnp.float32) * width * factor_of
    return jnp.minimum(jnp.maximum(result, -most), most).astype(dtype)


def setup_inputs(seed: int = 0) -> dict:
    streams_of = jax.random.split(jax.random.key(seed), 6)
    queries = normal_values(streams_of[0], (LAYERS, NQ, GRAD), 1.0, 6.0, ((0, 16), (1, 32)))
    train_grads = normal_values(streams_of[1], (LAYERS, NTRAIN, GRAD), GRAD ** -0.5, 0.09375, ((0, 16), (1, 32)))
    basis_in = normal_values(streams_of[2], (LAYERS, IN_DIM, IN_DIM), IN_DIM ** -0.5, 0.75, ((0, 16),), jnp.float32)
    basis_out = normal_values(streams_of[3], (LAYERS, OUT_DIM, OUT_DIM), OUT_DIM ** -0.5, 0.75, ((0, 16),), jnp.float32)
    inverse_eigen = jnp.clip(jnp.exp(math.log(1.0) - 2.9957323 * jax.random.uniform(streams_of[4], (LAYERS, OUT_DIM, IN_DIM), jnp.float32) ** levels(streams_of[4], (LAYERS, OUT_DIM, IN_DIM), ((0, 16),), -0.2, 0.2)), 0.05, 1.0)
    return {"queries": queries, "train_grads": train_grads, "basis_in": basis_in, "basis_out": basis_out, "inverse_eigen": inverse_eigen}


def precondition(block, basis_in, basis_out, inverse_eigen):
    count = block.shape[0]
    grads = block.astype(jnp.float32).reshape(count, OUT_DIM, IN_DIM)
    hp = lax.Precision.HIGHEST
    right = jnp.einsum("qoi,ia->qoa", grads, basis_in, precision=hp)
    rotated = jnp.einsum("ob,qoa->qba", basis_out, right, precision=hp)
    scaled = rotated * inverse_eigen[None]
    back = jnp.einsum("qba,ja->qbj", scaled, basis_in, precision=hp)
    full = jnp.einsum("ob,qbj->qoj", basis_out, back, precision=hp)
    return full.reshape(count, GRAD).astype(jnp.bfloat16)


def reference(queries, train_grads, basis_in, basis_out, inverse_eigen):
    total = jnp.zeros((NQ, NTRAIN), jnp.float32)
    for layer_id in range(LAYERS):
        conditioned = precondition(queries[layer_id], basis_in[layer_id], basis_out[layer_id], inverse_eigen[layer_id])
        total = total + lax.dot_general(conditioned, train_grads[layer_id], (((1,), (1,)), ((), ())), preferred_element_type=jnp.float32)
    return total
```

```python
import functools

import jax
import jax.numpy as jnp
from jax import lax
from jax.experimental import pallas as pl
from jax.experimental.pallas import tpu as pltpu
from jax.sharding import PartitionSpec as P

MESH = pl.DeviceIdType.MESH
NY, NH, NC = 8, 2, 2
NL, NZ = 2, 8
HALF = 16
WIDTH = 64
GRAD = WIDTH * WIDTH
LANES = 128
PAIRS = GRAD // LANES
BLOCK = 64
COLS = 512
F32, BF16 = jnp.float32, jnp.bfloat16


def split(value):
    high = value.astype(BF16)
    return high, (value - high.astype(F32)).astype(BF16)


def dot(left, right, dims=((1,), (0,))):
    return lax.dot_general(left, right, (dims, ((), ())), preferred_element_type=F32)


def twice(value):
    return jnp.concatenate([value, value], axis=1)


def lower_half(shape):
    return lax.rem(lax.broadcasted_iota(jnp.int32, shape, 1), LANES) < WIDTH


def weights(bi_ref, bo_ref, eig_ref):
    wide = twice(bi_ref[...])
    low = lower_half(wide.shape)
    diag = jnp.concatenate([jnp.where(low, wide, 0.0), jnp.where(low, 0.0, wide)], axis=0)
    diag_hi, diag_lo = split(diag)
    first = jnp.concatenate([diag_hi, diag_lo], axis=0)
    last = jnp.concatenate([diag_hi, diag_hi, diag_lo], axis=1)
    even, odd = bo_ref[pl.ds(0, PAIRS, stride=2), :], bo_ref[pl.ds(1, PAIRS, stride=2), :]
    rows = jnp.concatenate([even, odd], axis=1)
    rows_hi = rows.astype(BF16).astype(F32)
    rows_lo = rows - rows_hi
    into = jnp.transpose(jnp.concatenate([rows_hi, rows_hi, rows_lo, rows_lo], axis=0)).astype(BF16)
    stack = jnp.concatenate([even, odd], axis=0)
    stack_hi = stack.astype(BF16).astype(F32)
    back = jnp.concatenate([twice(stack_hi), twice(stack - stack_hi)], axis=1).astype(BF16)
    return first, into, twice(eig_ref[...]), back, last


def precondition(block, mats, rows_ref, turned_ref):
    first, into, eig, back, last = mats
    stacked = jnp.concatenate([block[:, p * LANES : (p + 1) * LANES] for p in range(PAIRS)], axis=0)
    rows_ref[...] = dot(jnp.concatenate([stacked, stacked], axis=1), first)
    right = jnp.concatenate([rows_ref[pl.ds(q, PAIRS, stride=HALF), :] for q in range(HALF)], axis=1)
    right_hi, right_lo = split(right)
    both = dot(into, jnp.concatenate([right_hi, right_lo, right_hi, right_lo], axis=0))
    low = lower_half((WIDTH, HALF * LANES))
    picked = jnp.where(low, both[:WIDTH], both[WIDTH:])
    scaled = []
    for q in range(HALF):
        part = picked[:, q * LANES : (q + 1) * LANES]
        scaled.append((part + pltpu.roll(part, WIDTH, 1)) * eig)
    scaled_hi, scaled_lo = split(jnp.concatenate(scaled, axis=1))
    left = dot(back, jnp.concatenate([scaled_hi, scaled_lo, scaled_hi, scaled_lo], axis=0))
    left = jnp.where(lower_half((PAIRS, HALF * LANES)), left[:PAIRS], left[PAIRS:])
    left = jnp.concatenate([left[:, q * LANES : (q + 1) * LANES] for q in range(HALF)], axis=0)
    left_hi, left_lo = split(left)
    full = dot(jnp.concatenate([left_hi, left_lo, left_hi], axis=1), last, ((1,), (1,)))
    for q in range(HALF):
        turned_ref[pl.ds(q, PAIRS, stride=HALF), :] = full[q * PAIRS : (q + 1) * PAIRS]
    return [turned_ref[p * HALF : (p + 1) * HALF, :].astype(BF16) for p in range(PAIRS)]


def kernel(
    q_hbm, t_hbm, bi_ref, bo_ref, eig_ref, out_ref,
    q_ref, t_ref, cond, outbox, inbox, xbox, sums, rows_ref, turned_ref,
    load_sem, y_send, y_recv, y4_send, y4_recv, x_send, x_recv, s_send, s_recv, z_send, z_recv, l_send, l_recv,
):
    ex, layer = lax.axis_index("ex"), lax.axis_index("layer")
    y, h, c = ex // (NH * NC), lax.rem(ex // NC, NH), lax.rem(ex, NC)
    lo, z = layer // NZ, lax.rem(layer, NZ)

    def device(yy, hh, cc, ll, zz):
        return ((yy * NH + hh) * NC + cc, ll * NZ + zz)

    y_next = device(lax.rem(y + 1, NY), h, c, lo, z)
    y_prev = device(lax.rem(y + NY - 1, NY), h, c, lo, z)
    x_peer = device(y, 1 - h, c, lo, z)
    sibling = device(y, h, 1 - c, lo, z)
    lo_peer = device(y, h, c, 1 - lo, z)

    loads = [
        pltpu.make_async_copy(q_hbm.at[0], q_ref, load_sem.at[0]),
        pltpu.make_async_copy(t_hbm.at[0], t_ref, load_sem.at[1]),
    ]
    for load in loads:
        load.start()

    barrier = pltpu.get_barrier_semaphore()
    for peer in (y_next, y_prev, x_peer, sibling, lo_peer):
        pl.semaphore_signal(barrier, inc=1, device_id=peer, device_id_type=MESH)

    def greet(k, _):
        pl.semaphore_signal(
            barrier, inc=1, device_id=device(y, h, c, lo, lax.rem(z + k, NZ)), device_id_type=MESH
        )
        return 0

    lax.fori_loop(1, NZ, greet, 0)

    def rows_at(place, hh, cc, half):
        start = ((place * NH + hh) * NC + cc) * (2 * HALF) + half * HALF
        return pl.ds(pl.multiple_of(start, HALF), HALF)

    def copy(rows, send, recv, peer):
        return pltpu.make_async_remote_copy(
            src_ref=cond.at[rows], dst_ref=cond.at[rows], send_sem=send, recv_sem=recv,
            device_id=peer, device_id_type=MESH,
        )

    def stream_rows(stream, place):
        return rows_at(place, 1 - h if stream == 2 else h, c, 0 if stream == 0 else 1)

    def y_copy(stream, up, step):
        src_place = 0 if isinstance(step, int) and step == 0 else 2 * step - 1 + up
        index = (step * 3 + stream) * 2 + up
        return pltpu.make_async_remote_copy(
            src_ref=cond.at[stream_rows(stream, src_place)],
            dst_ref=cond.at[stream_rows(stream, 2 * (step + 1) - 1 + up)],
            send_sem=y_send.at[index], recv_sem=y_recv.at[index],
            device_id=y_prev if up else y_next, device_id_type=MESH,
        )

    def y4_copy(stream):
        down = lax.rem(c + stream, 2)
        peer = lax.rem(y + jnp.where(down == 1, NY - 1, 1), NY)
        return pltpu.make_async_remote_copy(
            src_ref=cond.at[stream_rows(stream, 5 + down)], dst_ref=cond.at[stream_rows(stream, 7)],
            send_sem=y4_send.at[stream], recv_sem=y4_recv.at[stream],
            device_id=device(peer, h, c, lo, z), device_id_type=MESH,
        )

    def x_copy(place, own, half=0):
        index = place if half == 0 else NY
        return copy(rows_at(place, h if own else 1 - h, c, half), x_send.at[index], x_recv.at[index], x_peer)

    def s_copy(place, hh_own, half, own):
        hh = h if hh_own else 1 - h
        index = (place * NH + (0 if hh_own else 1)) * 2 + half
        return copy(rows_at(place, hh, c if own else 1 - c, half), s_send.at[index], s_recv.at[index], sibling)

    mats = weights(bi_ref, bo_ref, eig_ref)
    loads[0].wait()
    for half in range(2):
        pieces = precondition(q_ref[half * HALF : (half + 1) * HALF, :], mats, rows_ref, turned_ref)
        for p, piece in enumerate(pieces):
            cond[rows_at(0, h, c, half), p * LANES : (p + 1) * LANES] = piece
        if half == 0:
            pl.semaphore_wait(barrier, 12)
        else:
            x_copy(0, True, 1).start()
        y_copy(half, 0, 0).start()
        y_copy(half, 1, 0).start()
        if half == 0:
            x_copy(0, True).start()
        s_copy(0, True, half, True).start()
    x_copy(0, False, 1).wait_recv()
    y_copy(2, 0, 0).start()
    y_copy(2, 1, 0).start()
    s_copy(0, False, 1, True).start()
    x_copy(0, False).wait_recv()
    s_copy(0, False, 0, True).start()

    def z_copy(place, hh, zm, blk):
        return pltpu.make_async_remote_copy(
            src_ref=outbox.at[pl.ds(pl.multiple_of((place * NH + hh) * BLOCK, BLOCK), BLOCK)],
            dst_ref=inbox.at[blk, z],
            send_sem=z_send.at[place * NH + hh], recv_sem=z_recv.at[blk * NZ + z],
            device_id=device(y, h, c, lo, zm), device_id_type=MESH,
        )

    def owner(place, hh):
        if isinstance(place, int) and place == 0:
            from_y = y
        elif isinstance(place, int):
            from_y = lax.rem(y + 4, NY)
        else:
            step, down = (place + 1) // 2, lax.rem(place + 1, 2)
            from_y = lax.rem(y + jnp.where(down == 1, step, NY - step), NY)
        m = from_y * NH + hh
        return lax.rem(m, NZ), m // NZ

    def multiply(place, places):
        count = places * NH * BLOCK
        rows = pl.ds(pl.multiple_of(place * NH * BLOCK, BLOCK), count)
        outbox[rows, :] = dot(cond[rows, :], t_ref[...], ((1,), (1,))).astype(BF16)
        for k in range(places):
            for hh in range(NH):
                zm, blk = owner(place + k, hh)

                @pl.when(zm != z)
                def _():
                    z_copy(place + k, hh, zm, blk).start()

                @pl.when(zm == z)
                def _():
                    rows = pl.ds(pl.multiple_of(((place + k) * NH + hh) * BLOCK, BLOCK), BLOCK)
                    inbox[blk, z] = outbox[rows, :]

    def wait_sibling(place):
        for own_h in (True, False):
            for half in range(2):
                s_copy(place, own_h, half, False).wait_recv()

    loads[1].wait()
    wait_sibling(0)
    multiply(0, 1)

    for step in range(1, 4):
        for stream in range(3):
            for up in range(2):
                y_copy(stream, up, step - 1).wait_recv()
                if step < 3:
                    y_copy(stream, up, step).start()
            if step == 3:
                y4_copy(stream).start()
            for up in range(2):
                place = 2 * step - 1 + up
                if stream == 0:
                    x_copy(place, True).start()
                s_copy(place, stream != 2, 0 if stream == 0 else 1, True).start()
        for up in range(2):
            place = 2 * step - 1 + up
            x_copy(place, False).wait_recv()
            s_copy(place, False, 0, True).start()
        for up in range(2):
            wait_sibling(2 * step - 1 + up)
        multiply_at = jnp.int32(2 * step - 1)
        multiply(multiply_at, 2)

    for stream in range(3):
        y4_copy(stream).wait_recv()
        if stream == 0:
            x_copy(7, True).start()
        s_copy(7, stream != 2, 0 if stream == 0 else 1, True).start()
    x_copy(7, False).wait_recv()
    s_copy(7, False, 0, True).start()
    wait_sibling(7)
    multiply(7, 1)

    def collect(blk):
        def await_one(k, _):
            frm = lax.rem(z + k, NZ)
            pltpu.make_async_remote_copy(
                src_ref=inbox.at[blk, frm], dst_ref=inbox.at[blk, frm],
                send_sem=z_send.at[0], recv_sem=z_recv.at[blk * NZ + frm],
                device_id=device(y, h, c, lo, frm), device_id_type=MESH,
            ).wait_recv()
            return 0

        lax.fori_loop(1, NZ, await_one, 0)
        total = inbox[blk, 0].astype(F32)
        for k in range(1, NZ):
            total += inbox[blk, k].astype(F32)
        return total

    l_copy = pltpu.make_async_remote_copy(
        src_ref=sums, dst_ref=xbox, send_sem=l_send, recv_sem=l_recv, device_id=lo_peer, device_id_type=MESH
    )
    sums[...] = collect(1 - lo)
    l_copy.start()
    mine = collect(lo)
    l_copy.wait_recv()
    out_ref[...] = mine + xbox[...]

    l_copy.wait_send()
    for stream in range(3):
        for step in range(3):
            for up in range(2):
                y_copy(stream, up, step).wait_send()
        y4_copy(stream).wait_send()
    for place in range(NY):
        x_copy(place, True).wait_send()
        for own_h in (True, False):
            for half in range(2):
                s_copy(place, own_h, half, True).wait_send()
    x_copy(0, True, 1).wait_send()
    for place in range(NY):
        for hh in range(NH):
            zm, blk = owner(place if place in (0, 7) else jnp.int32(place), hh)

            @pl.when(zm != z)
            def _():
                z_copy(place, hh, zm, blk).wait_send()


def per_device(queries, train_grads, basis_in, basis_out, inverse_eigen):
    any_space = pl.BlockSpec(memory_space=pl.ANY)
    vmem = pl.BlockSpec(memory_space=pltpu.VMEM)
    dma = pltpu.SemaphoreType.DMA
    return pl.pallas_call(
        kernel,
        out_shape=jax.ShapeDtypeStruct((BLOCK, COLS), F32),
        in_specs=[any_space, any_space, vmem, vmem, vmem],
        out_specs=vmem,
        scratch_shapes=[
            pltpu.VMEM((2 * HALF, GRAD), BF16),
            pltpu.VMEM((COLS, GRAD), BF16),
            pltpu.VMEM((NY * NH * BLOCK, GRAD), BF16),
            pltpu.VMEM((NY * NH * BLOCK, COLS), BF16),
            pltpu.VMEM((NL, NZ, BLOCK, COLS), BF16),
            pltpu.VMEM((BLOCK, COLS), F32),
            pltpu.VMEM((BLOCK, COLS), F32),
            pltpu.VMEM((PAIRS * HALF, LANES), F32),
            pltpu.VMEM((PAIRS * HALF, LANES), F32),
            dma((2,)),
            dma((18,)), dma((18,)),
            dma((3,)), dma((3,)),
            dma((9,)), dma((9,)),
            dma((32,)), dma((32,)),
            dma((16,)), dma((16,)),
            dma, dma,
        ],
        compiler_params=pltpu.CompilerParams(
            collective_id=0, has_side_effects=True, vmem_limit_bytes=40 * 1024 * 1024
        ),
        cost_estimate=pl.CostEstimate(
            flops=2 * 1024 * GRAD * COLS, bytes_accessed=5 * 1024 * 1024, transcendentals=0
        ),
        name="influence",
    )(queries, train_grads, basis_in[0], basis_out[0], inverse_eigen[0])


def solution(mesh):
    in_specs = (
        P("layer", "ex", None),
        P("layer", "ex", None),
        P("layer", None, None),
        P("layer", None, None),
        P("layer", None, None),
    )
    out_specs = P("layer", "ex")
    return jax.shard_map(
        per_device, mesh=mesh, in_specs=in_specs, out_specs=out_specs, check_vma=False
    )
```

```python
import functools

import jax
import jax.numpy as jnp
from jax import lax
from jax.experimental import pallas as pl
from jax.experimental.pallas import tpu as pltpu
from jax.sharding import PartitionSpec as P

MESH = pl.DeviceIdType.MESH
NY, NH, NC = 8, 2, 2
NL, NZ = 2, 8
HALF = 16
WIDTH = 64
GRAD = WIDTH * WIDTH
LANES = 128
PAIRS = GRAD // LANES
BLOCK = 64
COLS = 512
F32, BF16 = jnp.float32, jnp.bfloat16


def split(value):
    high = value.astype(BF16)
    return high, (value - high.astype(F32)).astype(BF16)


def dot(left, right, dims=((1,), (0,))):
    return lax.dot_general(left, right, (dims, ((), ())), preferred_element_type=F32)


def twice(value):
    return jnp.concatenate([value, value], axis=1)


def lower_half(shape):
    return lax.rem(lax.broadcasted_iota(jnp.int32, shape, 1), LANES) < WIDTH


def weights(bi_ref, bo_ref, eig_ref):
    wide = twice(bi_ref[...])
    low = lower_half(wide.shape)
    diag = jnp.concatenate([jnp.where(low, wide, 0.0), jnp.where(low, 0.0, wide)], axis=0)
    diag_hi, diag_lo = split(diag)
    first = jnp.concatenate([diag_hi, diag_lo], axis=0)
    last = jnp.concatenate([diag_hi, diag_hi, diag_lo], axis=1)
    even, odd = bo_ref[pl.ds(0, PAIRS, stride=2), :], bo_ref[pl.ds(1, PAIRS, stride=2), :]
    rows = jnp.concatenate([even, odd], axis=1)
    rows_hi = rows.astype(BF16).astype(F32)
    rows_lo = rows - rows_hi
    into = jnp.transpose(jnp.concatenate([rows_hi, rows_hi, rows_lo, rows_lo], axis=0)).astype(BF16)
    stack = jnp.concatenate([even, odd], axis=0)
    stack_hi = stack.astype(BF16).astype(F32)
    back = jnp.concatenate([twice(stack_hi), twice(stack - stack_hi)], axis=1).astype(BF16)
    return first, into, twice(eig_ref[...]), back, last


def precondition(block, mats, rows_ref, turned_ref):
    first, into, eig, back, last = mats
    stacked = jnp.concatenate([block[:, p * LANES : (p + 1) * LANES] for p in range(PAIRS)], axis=0)
    rows_ref[...] = dot(jnp.concatenate([stacked, stacked], axis=1), first)
    right = jnp.concatenate([rows_ref[pl.ds(q, PAIRS, stride=HALF), :] for q in range(HALF)], axis=1)
    right_hi, right_lo = split(right)
    both = dot(into, jnp.concatenate([right_hi, right_lo, right_hi, right_lo], axis=0))
    low = lower_half((WIDTH, HALF * LANES))
    picked = jnp.where(low, both[:WIDTH], both[WIDTH:])
    scaled = []
    for q in range(HALF):
        part = picked[:, q * LANES : (q + 1) * LANES]
        scaled.append((part + pltpu.roll(part, WIDTH, 1)) * eig)
    scaled_hi, scaled_lo = split(jnp.concatenate(scaled, axis=1))
    left = dot(back, jnp.concatenate([scaled_hi, scaled_lo, scaled_hi, scaled_lo], axis=0))
    left = jnp.where(lower_half((PAIRS, HALF * LANES)), left[:PAIRS], left[PAIRS:])
    left = jnp.concatenate([left[:, q * LANES : (q + 1) * LANES] for q in range(HALF)], axis=0)
    left_hi, left_lo = split(left)
    full = dot(jnp.concatenate([left_hi, left_lo, left_hi], axis=1), last, ((1,), (1,)))
    for q in range(HALF):
        turned_ref[pl.ds(q, PAIRS, stride=HALF), :] = full[q * PAIRS : (q + 1) * PAIRS]
    return [turned_ref[p * HALF : (p + 1) * HALF, :].astype(BF16) for p in range(PAIRS)]


def kernel(
    q_hbm, t_hbm, bi_hbm, bo_hbm, eig_hbm, out_ref,
    q_ref, t_ref, bi_ref, bo_ref, eig_ref, cond, outbox, inbox, xbox, sums, rows_ref, turned_ref,
    load_sem, y_send, y_recv, y4_send, y4_recv, x_send, x_recv, s_send, s_recv, z_send, z_recv, l_send, l_recv,
):
    ex, layer = lax.axis_index("ex"), lax.axis_index("layer")
    y, h, c = ex // (NH * NC), lax.rem(ex // NC, NH), lax.rem(ex, NC)
    lo, z = layer // NZ, lax.rem(layer, NZ)

    def device(yy, hh, cc, ll, zz):
        return ((yy * NH + hh) * NC + cc, ll * NZ + zz)

    y_next = device(lax.rem(y + 1, NY), h, c, lo, z)
    y_prev = device(lax.rem(y + NY - 1, NY), h, c, lo, z)
    x_peer = device(y, 1 - h, c, lo, z)
    sibling = device(y, h, 1 - c, lo, z)
    lo_peer = device(y, h, c, 1 - lo, z)

    with jax.named_scope("greet"):
        barrier = pltpu.get_barrier_semaphore()
        for peer in (y_next, y_prev, x_peer, sibling, lo_peer):
            pl.semaphore_signal(barrier, inc=1, device_id=peer, device_id_type=MESH)

        def greet(k, _):
            pl.semaphore_signal(
                barrier, inc=1, device_id=device(y, h, c, lo, lax.rem(z + k, NZ)), device_id_type=MESH
            )
            return 0

        lax.fori_loop(1, NZ, greet, 0)
        pairs = [(q_hbm, q_ref), (bi_hbm, bi_ref), (bo_hbm, bo_ref), (eig_hbm, eig_ref), (t_hbm, t_ref)]
        loads = [pltpu.make_async_copy(src.at[0], dst, load_sem.at[i]) for i, (src, dst) in enumerate(pairs)]
        for load in loads:
            load.start()

    def place_rows(half, place, count):
        start = (half * NY + place) * (NH * NC * HALF)
        return pl.ds(start, count * NH * NC * HALF)

    def rows_at(place, hh, cc, half):
        start = (((half * NY + place) * NH + hh) * NC + cc) * HALF
        return pl.ds(pl.multiple_of(start, HALF), HALF)

    def copy(rows, send, recv, peer):
        return pltpu.make_async_remote_copy(
            src_ref=cond.at[rows], dst_ref=cond.at[rows], send_sem=send, recv_sem=recv,
            device_id=peer, device_id_type=MESH,
        )

    def stream_rows(stream, place):
        return rows_at(place, 1 - h if stream == 2 else h, c, 0 if stream == 0 else 1)

    def y_copy(stream, up, step):
        src_place = 0 if step == 0 else 2 * step - 1 + up
        index = (step * 3 + stream) * 2 + up
        return pltpu.make_async_remote_copy(
            src_ref=cond.at[stream_rows(stream, src_place)],
            dst_ref=cond.at[stream_rows(stream, 2 * (step + 1) - 1 + up)],
            send_sem=y_send.at[index], recv_sem=y_recv.at[index],
            device_id=y_prev if up else y_next, device_id_type=MESH,
        )

    def y4_copy(stream):
        down = lax.rem(c + stream, 2)
        peer = lax.rem(y + jnp.where(down == 1, NY - 1, 1), NY)
        return pltpu.make_async_remote_copy(
            src_ref=cond.at[stream_rows(stream, 5 + down)], dst_ref=cond.at[stream_rows(stream, 7)],
            send_sem=y4_send.at[stream], recv_sem=y4_recv.at[stream],
            device_id=device(peer, h, c, lo, z), device_id_type=MESH,
        )

    def x_copy(place, own, half=0):
        index = place if half == 0 else NY
        return copy(rows_at(place, h if own else 1 - h, c, half), x_send.at[index], x_recv.at[index], x_peer)

    def s_copy(place, hh_own, half, own):
        hh = h if hh_own else 1 - h
        index = (place * NH + (0 if hh_own else 1)) * 2 + half
        return copy(rows_at(place, hh, c if own else 1 - c, half), s_send.at[index], s_recv.at[index], sibling)

    def z_copy(half, place, hh, zm, blk):
        index = (half * NY + place) * NH + hh
        rows = pl.ds(pl.multiple_of(index * (NC * HALF), NC * HALF), NC * HALF)
        return pltpu.make_async_remote_copy(
            src_ref=outbox.at[rows], dst_ref=inbox.at[blk, half, z],
            send_sem=z_send.at[index], recv_sem=z_recv.at[(blk * 2 + half) * NZ + z],
            device_id=device(y, h, c, lo, zm), device_id_type=MESH,
        )

    def owner(place, hh):
        shift = (0, 7, 1, 6, 2, 5, 3, 4)[place]
        m = lax.rem(y + shift, NY) * NH + hh
        return lax.rem(m, NZ), m // NZ

    def wait_sibling(half, place):
        for hh_own in (True, False):
            s_copy(place, hh_own, half, False).wait_recv()

    def multiply(half, place, places):
        with jax.named_scope(f"await_{half}_{place}"):
            for k in range(places):
                wait_sibling(half, place + k)
        with jax.named_scope(f"multiply_{half}_{place}"):
            rows = place_rows(half, place, places)
            outbox[rows, :] = dot(cond[rows, :], t_ref[...], ((1,), (1,))).astype(BF16)
            for k in range(places):
                for hh in range(NH):
                    zm, blk = owner(place + k, hh)

                    @pl.when(zm != z)
                    def _():
                        z_copy(half, place + k, hh, zm, blk).start()

                    @pl.when(zm == z)
                    def _():
                        start = ((half * NY + place + k) * NH + hh) * (NC * HALF)
                        inbox[blk, half, z] = outbox[start : start + NC * HALF, :]

    def arrive(stream, step):
        with jax.named_scope(f"y_{stream}_{step}"):
            for up in range(2):
                y_copy(stream, up, step - 1).wait_recv()
                if step < 3:
                    y_copy(stream, up, step).start()
            if step == 3:
                y4_copy(stream).start()
            for up in range(2):
                place = 2 * step - 1 + up
                if stream == 0:
                    x_copy(place, True).start()
                s_copy(place, stream != 2, 0 if stream == 0 else 1, True).start()

    def arrive_far(stream):
        with jax.named_scope(f"y_{stream}_4"):
            y4_copy(stream).wait_recv()
            if stream == 0:
                x_copy(7, True).start()
            s_copy(7, stream != 2, 0 if stream == 0 else 1, True).start()

    def arrive_x(*places):
        with jax.named_scope(f"x_{places[0]}"):
            for place in places:
                x_copy(place, False).wait_recv()
                s_copy(place, False, 0, True).start()

    def condition(half):
        pieces = precondition(q_ref[half * HALF : (half + 1) * HALF, :], mats, rows_ref, turned_ref)
        for p, piece in enumerate(pieces):
            cond[rows_at(0, h, c, half), p * LANES : (p + 1) * LANES] = piece

    with jax.named_scope("load"):
        for load in loads[:4]:
            load.wait()
    with jax.named_scope("condition_0"):
        mats = weights(bi_ref, bo_ref, eig_ref)
        condition(0)
    with jax.named_scope("barrier"):
        pl.semaphore_wait(barrier, 12)
    y_copy(0, 0, 0).start()
    y_copy(0, 1, 0).start()
    with jax.named_scope("condition_1"):
        condition(1)
    x_copy(0, True, 1).start()
    y_copy(1, 0, 0).start()
    y_copy(1, 1, 0).start()
    x_copy(0, True).start()
    s_copy(0, True, 0, True).start()
    s_copy(0, True, 1, True).start()
    with jax.named_scope("x_other"):
        x_copy(0, False, 1).wait_recv()
    y_copy(2, 0, 0).start()
    y_copy(2, 1, 0).start()
    s_copy(0, False, 1, True).start()
    arrive_x(0)
    with jax.named_scope("load_train"):
        loads[4].wait()

    for step in range(1, 4):
        place, places = (2 * step - 3, 2) if step > 1 else (0, 1)
        arrive(0, step)
        multiply(0, place, places)
        arrive(1, step)
        multiply(1, place, places)
        arrive(2, step)
        arrive_x(2 * step - 1, 2 * step)
    arrive_far(0)
    multiply(0, 5, 2)
    arrive_far(1)
    arrive_far(2)
    multiply(1, 5, 2)
    arrive_x(7)
    multiply(0, 7, 1)
    multiply(1, 7, 1)

    with jax.named_scope("drain"):
        for stream in range(3):
            for step in range(3):
                for up in range(2):
                    y_copy(stream, up, step).wait_send()
            y4_copy(stream).wait_send()
        for place in range(NY):
            x_copy(place, True).wait_send()
            for hh_own in (True, False):
                for half in range(2):
                    s_copy(place, hh_own, half, True).wait_send()
        x_copy(0, True, 1).wait_send()

    def collect(blk, half):
        def await_one(k, _):
            frm = lax.rem(z + k, NZ)
            pltpu.make_async_remote_copy(
                src_ref=inbox.at[blk, half, frm], dst_ref=inbox.at[blk, half, frm],
                send_sem=z_send.at[0], recv_sem=z_recv.at[(blk * 2 + half) * NZ + frm],
                device_id=device(y, h, c, lo, frm), device_id_type=MESH,
            ).wait_recv()
            return 0

        lax.fori_loop(1, NZ, await_one, 0)
        total = inbox[blk, half, 0].astype(F32)
        for k in range(1, NZ):
            total += inbox[blk, half, k].astype(F32)
        return total

    def l_copy(half):
        return pltpu.make_async_remote_copy(
            src_ref=sums.at[half], dst_ref=xbox.at[half], send_sem=l_send.at[half], recv_sem=l_recv.at[half],
            device_id=lo_peer, device_id_type=MESH,
        )

    with jax.named_scope("collect_other"):
        for half in range(2):
            sums[half] = collect(1 - lo, half)
            l_copy(half).start()
    with jax.named_scope("collect_own"):
        mine = [collect(lo, half) for half in range(2)]
    with jax.named_scope("finish"):
        for half in range(2):
            l_copy(half).wait_recv()
            total = mine[half] + xbox[half]
            for cc in range(NC):
                out_ref[(cc * 2 + half) * HALF : (cc * 2 + half + 1) * HALF, :] = total[cc * HALF : (cc + 1) * HALF]
    with jax.named_scope("drain_sums"):
        for half in range(2):
            l_copy(half).wait_send()
            for place in range(NY):
                for hh in range(NH):
                    zm, blk = owner(place, hh)

                    @pl.when(zm != z)
                    def _():
                        z_copy(half, place, hh, zm, blk).wait_send()


def per_device(queries, train_grads, basis_in, basis_out, inverse_eigen):
    any_space = pl.BlockSpec(memory_space=pl.ANY)
    vmem = pl.BlockSpec(memory_space=pltpu.VMEM)
    dma = pltpu.SemaphoreType.DMA
    return pl.pallas_call(
        kernel,
        out_shape=jax.ShapeDtypeStruct((BLOCK, COLS), F32),
        in_specs=[any_space] * 5,
        out_specs=vmem,
        scratch_shapes=[
            pltpu.VMEM((2 * HALF, GRAD), BF16),
            pltpu.VMEM((COLS, GRAD), BF16),
            pltpu.VMEM((WIDTH, WIDTH), F32),
            pltpu.VMEM((WIDTH, WIDTH), F32),
            pltpu.VMEM((WIDTH, WIDTH), F32),
            pltpu.VMEM((NY * NH * BLOCK, GRAD), BF16),
            pltpu.VMEM((NY * NH * BLOCK, COLS), BF16),
            pltpu.VMEM((NL, 2, NZ, NC * HALF, COLS), BF16),
            pltpu.VMEM((2, NC * HALF, COLS), F32),
            pltpu.VMEM((2, NC * HALF, COLS), F32),
            pltpu.VMEM((PAIRS * HALF, LANES), F32),
            pltpu.VMEM((PAIRS * HALF, LANES), F32),
            dma((5,)),
            dma((18,)), dma((18,)),
            dma((3,)), dma((3,)),
            dma((9,)), dma((9,)),
            dma((32,)), dma((32,)),
            dma((32,)), dma((32,)),
            dma((2,)), dma((2,)),
        ],
        compiler_params=pltpu.CompilerParams(
            collective_id=0, has_side_effects=True, vmem_limit_bytes=60 * 1024 * 1024
        ),
        cost_estimate=pl.CostEstimate(
            flops=2 * 1024 * GRAD * COLS, bytes_accessed=5 * 1024 * 1024, transcendentals=0
        ),
        name="influence",
    )(queries, train_grads, basis_in, basis_out, inverse_eigen)


def solution(mesh):
    in_specs = (
        P("layer", "ex", None),
        P("layer", "ex", None),
        P("layer", None, None),
        P("layer", None, None),
        P("layer", None, None),
    )
    out_specs = P("layer", "ex")
    return jax.shard_map(
        per_device, mesh=mesh, in_specs=in_specs, out_specs=out_specs, check_vma=False
    )
```

```python
import functools

import jax
import jax.numpy as jnp
from jax import lax
from jax.experimental import pallas as pl
from jax.experimental.pallas import tpu as pltpu
from jax.sharding import PartitionSpec as P

MESH = pl.DeviceIdType.MESH
NY, NH, NC = 8, 2, 2
NL, NZ = 2, 8
HALF = 16
WIDTH = 64
GRAD = WIDTH * WIDTH
LANES = 128
PAIRS = GRAD // LANES
BLOCK = 64
COLS = 512
F32, BF16 = jnp.float32, jnp.bfloat16


def split(value):
    high = value.astype(BF16)
    return high, (value - high.astype(F32)).astype(BF16)


def dot(left, right, dims=((1,), (0,))):
    return lax.dot_general(left, right, (dims, ((), ())), preferred_element_type=F32)


def twice(value):
    return jnp.concatenate([value, value], axis=1)


def lower_half(shape):
    return lax.rem(lax.broadcasted_iota(jnp.int32, shape, 1), LANES) < WIDTH


def weights(bi_ref, bo_ref, eig_ref):
    wide = twice(bi_ref[...])
    low = lower_half(wide.shape)
    diag = jnp.concatenate([jnp.where(low, wide, 0.0), jnp.where(low, 0.0, wide)], axis=0)
    diag_hi, diag_lo = split(diag)
    first = jnp.concatenate([diag_hi, diag_lo], axis=0)
    last = jnp.concatenate([diag_hi, diag_hi, diag_lo], axis=1)
    even, odd = bo_ref[pl.ds(0, PAIRS, stride=2), :], bo_ref[pl.ds(1, PAIRS, stride=2), :]
    rows = jnp.concatenate([even, odd], axis=1)
    rows_hi = rows.astype(BF16).astype(F32)
    rows_lo = rows - rows_hi
    into = jnp.transpose(jnp.concatenate([rows_hi, rows_hi, rows_lo, rows_lo], axis=0)).astype(BF16)
    stack = jnp.concatenate([even, odd], axis=0)
    stack_hi = stack.astype(BF16).astype(F32)
    back = jnp.concatenate([twice(stack_hi), twice(stack - stack_hi)], axis=1).astype(BF16)
    return first, into, twice(eig_ref[...]), back, last


def precondition(block, mats, rows_ref, turned_ref):
    first, into, eig, back, last = mats
    stacked = jnp.concatenate([block[:, p * LANES : (p + 1) * LANES] for p in range(PAIRS)], axis=0)
    rows_ref[...] = dot(jnp.concatenate([stacked, stacked], axis=1), first)
    right = jnp.concatenate([rows_ref[pl.ds(q, PAIRS, stride=HALF), :] for q in range(HALF)], axis=1)
    right_hi, right_lo = split(right)
    both = dot(into, jnp.concatenate([right_hi, right_lo, right_hi, right_lo], axis=0))
    low = lower_half((WIDTH, HALF * LANES))
    picked = jnp.where(low, both[:WIDTH], both[WIDTH:])
    scaled = []
    for q in range(HALF):
        part = picked[:, q * LANES : (q + 1) * LANES]
        scaled.append((part + pltpu.roll(part, WIDTH, 1)) * eig)
    scaled_hi, scaled_lo = split(jnp.concatenate(scaled, axis=1))
    left = dot(back, jnp.concatenate([scaled_hi, scaled_lo, scaled_hi, scaled_lo], axis=0))
    left = jnp.where(lower_half((PAIRS, HALF * LANES)), left[:PAIRS], left[PAIRS:])
    left = jnp.concatenate([left[:, q * LANES : (q + 1) * LANES] for q in range(HALF)], axis=0)
    left_hi, left_lo = split(left)
    full = dot(jnp.concatenate([left_hi, left_lo, left_hi], axis=1), last, ((1,), (1,)))
    for q in range(HALF):
        turned_ref[pl.ds(q, PAIRS, stride=HALF), :] = full[q * PAIRS : (q + 1) * PAIRS]
    return [turned_ref[p * HALF : (p + 1) * HALF, :].astype(BF16) for p in range(PAIRS)]


def kernel(
    q_hbm, t_hbm, bi_hbm, bo_hbm, eig_hbm, out_ref,
    q_ref, t_ref, bi_ref, bo_ref, eig_ref, cond, outbox, inbox, xbox, sums, rows_ref, turned_ref,
    load_sem, y_send, y_recv, y4_send, y4_recv, x_send, x_recv, s_send, s_recv, z_send, z_recv, l_send, l_recv,
):
    ex, layer = lax.axis_index("ex"), lax.axis_index("layer")
    y, h, c = ex // (NH * NC), lax.rem(ex // NC, NH), lax.rem(ex, NC)
    lo, z = layer // NZ, lax.rem(layer, NZ)

    def device(yy, hh, cc, ll, zz):
        return ((yy * NH + hh) * NC + cc, ll * NZ + zz)

    y_next = device(lax.rem(y + 1, NY), h, c, lo, z)
    y_prev = device(lax.rem(y + NY - 1, NY), h, c, lo, z)
    x_peer = device(y, 1 - h, c, lo, z)
    sibling = device(y, h, 1 - c, lo, z)
    lo_peer = device(y, h, c, 1 - lo, z)

    with jax.named_scope("greet"):
        pairs = [(q_hbm, q_ref), (bi_hbm, bi_ref), (bo_hbm, bo_ref), (eig_hbm, eig_ref), (t_hbm, t_ref)]
        loads = [pltpu.make_async_copy(src.at[0], dst, load_sem.at[i]) for i, (src, dst) in enumerate(pairs)]
        for load in loads[:4]:
            load.start()
        barrier = pltpu.get_barrier_semaphore()
        for peer in (y_next, y_prev, x_peer, sibling, lo_peer):
            pl.semaphore_signal(barrier, inc=1, device_id=peer, device_id_type=MESH)
        loads[4].start()
        for k in range(1, NZ):
            pl.semaphore_signal(
                barrier, inc=1, device_id=device(y, h, c, lo, lax.rem(z + k, NZ)), device_id_type=MESH
            )

    def place_rows(half, place, count):
        start = (half * NY + place) * (NH * NC * HALF)
        return pl.ds(start, count * NH * NC * HALF)

    def rows_at(place, hh, cc, half):
        start = (((half * NY + place) * NH + hh) * NC + cc) * HALF
        return pl.ds(pl.multiple_of(start, HALF), HALF)

    def copy(rows, send, recv, peer):
        return pltpu.make_async_remote_copy(
            src_ref=cond.at[rows], dst_ref=cond.at[rows], send_sem=send, recv_sem=recv,
            device_id=peer, device_id_type=MESH,
        )

    def stream_rows(stream, place):
        return rows_at(place, 1 - h if stream == 2 else h, c, 0 if stream == 0 else 1)

    def y_copy(stream, up, step):
        src_place = 0 if step == 0 else 2 * step - 1 + up
        index = (step * 3 + stream) * 2 + up
        return pltpu.make_async_remote_copy(
            src_ref=cond.at[stream_rows(stream, src_place)],
            dst_ref=cond.at[stream_rows(stream, 2 * (step + 1) - 1 + up)],
            send_sem=y_send.at[index], recv_sem=y_recv.at[index],
            device_id=y_prev if up else y_next, device_id_type=MESH,
        )

    def y4_copy(stream):
        down = lax.rem(c + stream, 2)
        peer = lax.rem(y + jnp.where(down == 1, NY - 1, 1), NY)
        return pltpu.make_async_remote_copy(
            src_ref=cond.at[stream_rows(stream, 5 + down)], dst_ref=cond.at[stream_rows(stream, 7)],
            send_sem=y4_send.at[stream], recv_sem=y4_recv.at[stream],
            device_id=device(peer, h, c, lo, z), device_id_type=MESH,
        )

    def x_copy(place, own, half=0):
        index = place if half == 0 else NY
        return copy(rows_at(place, h if own else 1 - h, c, half), x_send.at[index], x_recv.at[index], x_peer)

    def s_copy(place, hh_own, half, own):
        hh = h if hh_own else 1 - h
        index = (place * NH + (0 if hh_own else 1)) * 2 + half
        return copy(rows_at(place, hh, c if own else 1 - c, half), s_send.at[index], s_recv.at[index], sibling)

    def z_copy(half, place, hh, zm, blk):
        index = (half * NY + place) * NH + hh
        rows = pl.ds(pl.multiple_of(index * (NC * HALF), NC * HALF), NC * HALF)
        return pltpu.make_async_remote_copy(
            src_ref=outbox.at[rows], dst_ref=inbox.at[blk, half, z],
            send_sem=z_send.at[index], recv_sem=z_recv.at[(blk * 2 + half) * NZ + z],
            device_id=device(y, h, c, lo, zm), device_id_type=MESH,
        )

    def owner(place, hh):
        shift = (0, 7, 1, 6, 2, 5, 3, 4)[place]
        m = lax.rem(y + shift, NY) * NH + hh
        return lax.rem(m, NZ), m // NZ

    def multiply(half, place, places, hh_own=None):
        with jax.named_scope(f"await_{half}_{place}"):
            for k in range(places):
                for own in (True, False) if hh_own is None else (hh_own,):
                    s_copy(place + k, own, half, False).wait_recv()
        with jax.named_scope(f"multiply_{half}_{place}"):
            if hh_own is None:
                rows, parts = place_rows(half, place, places), range(NH)
            else:
                parts = (h if hh_own else 1 - h,)
                start = ((half * NY + place) * NH + parts[0]) * (NC * HALF)
                rows = pl.ds(pl.multiple_of(start, NC * HALF), NC * HALF)
            outbox[rows, :] = dot(cond[rows, :], t_ref[...], ((1,), (1,))).astype(BF16)
            for k in range(places):
                for hh in parts:
                    zm, blk = owner(place + k, hh)

                    @pl.when(zm != z)
                    def _():
                        z_copy(half, place + k, hh, zm, blk).start()

                    @pl.when(zm == z)
                    def _():
                        start = pl.multiple_of(((half * NY + place + k) * NH + hh) * (NC * HALF), NC * HALF)
                        inbox[blk, half, z] = outbox[pl.ds(start, NC * HALF), :]

    def multiply_both(place, places):
        for half in range(2):
            for k in range(places):
                for own in (True, False):
                    s_copy(place + k, own, half, False).wait_recv()
        count = places * NH * NC * HALF
        rows = [place_rows(half, place, places) for half in range(2)]
        product = dot(jnp.concatenate([cond[r, :] for r in rows], axis=0), t_ref[...], ((1,), (1,))).astype(BF16)
        for half in range(2):
            outbox[rows[half], :] = product[half * count : (half + 1) * count]
        for half in range(2):
            for k in range(places):
                for hh in range(NH):
                    zm, blk = owner(place + k, hh)

                    @pl.when(zm != z)
                    def _():
                        z_copy(half, place + k, hh, zm, blk).start()

                    @pl.when(zm == z)
                    def _():
                        start = pl.multiple_of(((half * NY + place + k) * NH + hh) * (NC * HALF), NC * HALF)
                        inbox[blk, half, z] = outbox[pl.ds(start, NC * HALF), :]

    def arrive(stream, step):
        with jax.named_scope(f"y_{stream}_{step}"):
            for up in range(2):
                y_copy(stream, up, step - 1).wait_recv()
                if step < 3:
                    y_copy(stream, up, step).start()
            if step == 3:
                y4_copy(stream).start()
            for up in range(2):
                place = 2 * step - 1 + up
                if stream == 0:
                    x_copy(place, True).start()
                s_copy(place, stream != 2, 0 if stream == 0 else 1, True).start()

    def arrive_far(stream):
        with jax.named_scope(f"y_{stream}_4"):
            y4_copy(stream).wait_recv()
            if stream == 0:
                x_copy(7, True).start()
            s_copy(7, stream != 2, 0 if stream == 0 else 1, True).start()

    def arrive_x(*places):
        with jax.named_scope(f"x_{places[0]}"):
            for place in places:
                x_copy(place, False).wait_recv()
                s_copy(place, False, 0, True).start()

    def condition(half):
        pieces = precondition(q_ref[half * HALF : (half + 1) * HALF, :], mats, rows_ref, turned_ref)
        for p, piece in enumerate(pieces):
            cond[rows_at(0, h, c, half), p * LANES : (p + 1) * LANES] = piece

    with jax.named_scope("load"):
        for load in loads[:4]:
            load.wait()
    with jax.named_scope("condition_0"):
        mats = weights(bi_ref, bo_ref, eig_ref)
        condition(0)
    with jax.named_scope("barrier"):
        pl.semaphore_wait(barrier, 12)
    y_copy(0, 0, 0).start()
    y_copy(0, 1, 0).start()
    with jax.named_scope("condition_1"):
        condition(1)
    x_copy(0, True, 1).start()
    y_copy(1, 0, 0).start()
    y_copy(1, 1, 0).start()
    x_copy(0, True).start()
    s_copy(0, True, 0, True).start()
    s_copy(0, True, 1, True).start()
    arrive(0, 1)
    with jax.named_scope("x_other"):
        x_copy(0, False, 1).wait_recv()
    y_copy(2, 0, 0).start()
    y_copy(2, 1, 0).start()
    s_copy(0, False, 1, True).start()
    arrive_x(0)
    with jax.named_scope("load_train"):
        loads[4].wait()
    multiply_both(0, 1)
    arrive(0, 2)
    arrive(1, 1)
    arrive(2, 1)
    arrive_x(1, 2)
    multiply_both(1, 2)
    arrive(0, 3)
    arrive(1, 2)
    arrive_x(3, 4)
    multiply(0, 3, 2)
    arrive_far(0)
    arrive(2, 2)
    multiply(1, 3, 2)
    arrive_x(5, 6)
    arrive(1, 3)
    multiply(0, 5, 2)
    arrive(2, 3)
    arrive_x(7)
    multiply(0, 7, 1)
    multiply(1, 5, 2)
    arrive_far(1)
    arrive_far(2)
    multiply(1, 7, 1)

    with jax.named_scope("drain"):
        for stream in range(3):
            for step in range(3):
                for up in range(2):
                    y_copy(stream, up, step).wait_send()
            y4_copy(stream).wait_send()
        for place in range(NY):
            x_copy(place, True).wait_send()
            for hh_own in (True, False):
                for half in range(2):
                    s_copy(place, hh_own, half, True).wait_send()
        x_copy(0, True, 1).wait_send()

    def collect(blk, half):
        def await_one(k, _):
            frm = lax.rem(z + k, NZ)
            pltpu.make_async_remote_copy(
                src_ref=inbox.at[blk, half, frm], dst_ref=inbox.at[blk, half, frm],
                send_sem=z_send.at[0], recv_sem=z_recv.at[(blk * 2 + half) * NZ + frm],
                device_id=device(y, h, c, lo, frm), device_id_type=MESH,
            ).wait_recv()
            return 0

        lax.fori_loop(1, NZ, await_one, 0)
        total = inbox[blk, half, 0].astype(F32)
        for k in range(1, NZ):
            total += inbox[blk, half, k].astype(F32)
        return total

    def l_copy(half):
        return pltpu.make_async_remote_copy(
            src_ref=sums.at[half], dst_ref=xbox.at[half], send_sem=l_send.at[half], recv_sem=l_recv.at[half],
            device_id=lo_peer, device_id_type=MESH,
        )

    mine = []
    for half in range(2):
        with jax.named_scope("collect_other"):
            sums[half] = collect(1 - lo, half)
            l_copy(half).start()
        with jax.named_scope("collect_own"):
            mine.append(collect(lo, half))
    with jax.named_scope("finish"):
        for half in range(2):
            l_copy(half).wait_recv()
            total = mine[half] + xbox[half]
            for cc in range(NC):
                out_ref[(cc * 2 + half) * HALF : (cc * 2 + half + 1) * HALF, :] = total[cc * HALF : (cc + 1) * HALF]
    with jax.named_scope("drain_sums"):
        for half in range(2):
            l_copy(half).wait_send()
            for place in range(NY):
                for hh in range(NH):
                    zm, blk = owner(place, hh)

                    @pl.when(zm != z)
                    def _():
                        z_copy(half, place, hh, zm, blk).wait_send()


def per_device(queries, train_grads, basis_in, basis_out, inverse_eigen):
    hbm = pl.BlockSpec(memory_space=pl.ANY)
    vmem = pl.BlockSpec(memory_space=pltpu.VMEM)
    dma = pltpu.SemaphoreType.DMA
    return pl.pallas_call(
        kernel,
        out_shape=jax.ShapeDtypeStruct((BLOCK, COLS), F32),
        in_specs=[hbm] * 5,
        out_specs=vmem,
        scratch_shapes=[
            pltpu.VMEM((2 * HALF, GRAD), BF16),
            pltpu.VMEM((COLS, GRAD), BF16),
            pltpu.VMEM((WIDTH, WIDTH), F32),
            pltpu.VMEM((WIDTH, WIDTH), F32),
            pltpu.VMEM((WIDTH, WIDTH), F32),
            pltpu.VMEM((NY * NH * BLOCK, GRAD), BF16),
            pltpu.VMEM((NY * NH * BLOCK, COLS), BF16),
            pltpu.VMEM((NL, 2, NZ, NC * HALF, COLS), BF16),
            pltpu.VMEM((2, NC * HALF, COLS), F32),
            pltpu.VMEM((2, NC * HALF, COLS), F32),
            pltpu.VMEM((PAIRS * HALF, LANES), F32),
            pltpu.VMEM((PAIRS * HALF, LANES), F32),
            dma((5,)),
            dma((18,)), dma((18,)),
            dma((3,)), dma((3,)),
            dma((9,)), dma((9,)),
            dma((32,)), dma((32,)),
            dma((32,)), dma((32,)),
            dma((2,)), dma((2,)),
        ],
        compiler_params=pltpu.CompilerParams(
            collective_id=0, has_side_effects=True, vmem_limit_bytes=60 * 1024 * 1024
        ),
        cost_estimate=pl.CostEstimate(
            flops=2 * 1024 * GRAD * COLS, bytes_accessed=5 * 1024 * 1024, transcendentals=0
        ),
        name="influence",
    )(queries, train_grads, basis_in, basis_out, inverse_eigen)


def solution(mesh):
    in_specs = (
        P("layer", "ex", None),
        P("layer", "ex", None),
        P("layer", None, None),
        P("layer", None, None),
        P("layer", None, None),
    )
    out_specs = P("layer", "ex")
    return jax.shard_map(
        per_device, mesh=mesh, in_specs=in_specs, out_specs=out_specs, check_vma=False
    )
```

```python
import functools

import jax
import jax.numpy as jnp
from jax import lax
from jax.experimental import pallas as pl
from jax.experimental.pallas import tpu as pltpu
from jax.sharding import PartitionSpec as P

MESH = pl.DeviceIdType.MESH
NY, NH, NC = 8, 2, 2
NL, NZ = 2, 8
HALF = 16
WIDTH = 64
GRAD = WIDTH * WIDTH
LANES = 128
PAIRS = GRAD // LANES
BLOCK = 64
COLS = 512
TURN = 256
SHIFTS = (0, 7, 1, 6, 2, 5, 3, 4)
F32, BF16 = jnp.float32, jnp.bfloat16


def split(value):
    high = value.astype(BF16)
    return high, (value - high.astype(F32)).astype(BF16)


def dot(left, right, dims=((1,), (0,))):
    return lax.dot_general(left, right, (dims, ((), ())), preferred_element_type=F32)


def twice(value):
    return jnp.concatenate([value, value], axis=1)


def lower_half(shape):
    return lax.rem(lax.broadcasted_iota(jnp.int32, shape, 1), LANES) < WIDTH


def weights(bi_ref, bo_ref, eig_ref):
    wide = twice(bi_ref[...])
    low = lower_half(wide.shape)
    diag = jnp.concatenate([jnp.where(low, wide, 0.0), jnp.where(low, 0.0, wide)], axis=0)
    diag_hi, diag_lo = split(diag)
    first = jnp.concatenate([diag_hi, diag_lo], axis=0)
    last = jnp.concatenate([diag_hi, diag_hi, diag_lo], axis=1)
    even, odd = bo_ref[pl.ds(0, PAIRS, stride=2), :], bo_ref[pl.ds(1, PAIRS, stride=2), :]
    rows = jnp.concatenate([even, odd], axis=1)
    rows_hi = rows.astype(BF16).astype(F32)
    rows_lo = rows - rows_hi
    into = jnp.transpose(jnp.concatenate([rows_hi, rows_hi, rows_lo, rows_lo], axis=0)).astype(BF16)
    stack = jnp.concatenate([even, odd], axis=0)
    stack_hi = stack.astype(BF16).astype(F32)
    back = jnp.concatenate([twice(stack_hi), twice(stack - stack_hi)], axis=1).astype(BF16)
    return first, into, twice(eig_ref[...]), back, last


def precondition(block, mats, rows_ref, turned_ref):
    first, into, eig, back, last = mats
    stacked = jnp.concatenate([block[:, p * LANES : (p + 1) * LANES] for p in range(PAIRS)], axis=0)
    rows_ref[...] = dot(jnp.concatenate([stacked, stacked], axis=1), first)
    right = jnp.concatenate([rows_ref[pl.ds(q, PAIRS, stride=HALF), :] for q in range(HALF)], axis=1)
    right_hi, right_lo = split(right)
    both = dot(into, jnp.concatenate([right_hi, right_lo, right_hi, right_lo], axis=0))
    low = lower_half((WIDTH, HALF * LANES))
    picked = jnp.where(low, both[:WIDTH], both[WIDTH:])
    scaled = []
    for q in range(HALF):
        part = picked[:, q * LANES : (q + 1) * LANES]
        scaled.append((part + pltpu.roll(part, WIDTH, 1)) * eig)
    scaled_hi, scaled_lo = split(jnp.concatenate(scaled, axis=1))
    left = dot(back, jnp.concatenate([scaled_hi, scaled_lo, scaled_hi, scaled_lo], axis=0))
    left = jnp.where(lower_half((PAIRS, HALF * LANES)), left[:PAIRS], left[PAIRS:])
    left = jnp.concatenate([left[:, q * LANES : (q + 1) * LANES] for q in range(HALF)], axis=0)
    left_hi, left_lo = split(left)
    full = dot(jnp.concatenate([left_hi, left_lo, left_hi], axis=1), last, ((1,), (1,)))
    for q in range(HALF):
        turned_ref[pl.ds(q, PAIRS, stride=HALF), :] = full[q * PAIRS : (q + 1) * PAIRS]
    return [turned_ref[p * HALF : (p + 1) * HALF, :].astype(BF16) for p in range(PAIRS)]


def kernel(
    q_hbm, t_hbm, bi_hbm, bo_hbm, eig_hbm, out_ref,
    q_ref, t_ref, turned_t, bi_ref, bo_ref, eig_ref, cond, outbox, inbox, xbox, sums, rows_ref, turned_ref,
    load_sem, y_send, y_recv, y4_send, y4_recv, x_send, x_recv, s_send, s_recv, z_send, z_recv, l_send, l_recv,
):
    ex, layer = lax.axis_index("ex"), lax.axis_index("layer")
    y, h, c = ex // (NH * NC), lax.rem(ex // NC, NH), lax.rem(ex, NC)
    lo, z = layer // NZ, lax.rem(layer, NZ)

    def device(yy, hh, cc, ll, zz):
        return ((yy * NH + hh) * NC + cc, ll * NZ + zz)

    y_next = device(lax.rem(y + 1, NY), h, c, lo, z)
    y_prev = device(lax.rem(y + NY - 1, NY), h, c, lo, z)
    x_peer = device(y, 1 - h, c, lo, z)
    sibling = device(y, h, 1 - c, lo, z)
    lo_peer = device(y, h, c, 1 - lo, z)

    with jax.named_scope("greet"):
        pairs = [(q_hbm, q_ref), (bi_hbm, bi_ref), (bo_hbm, bo_ref), (eig_hbm, eig_ref), (t_hbm, t_ref)]
        loads = [pltpu.make_async_copy(src.at[0], dst, load_sem.at[i]) for i, (src, dst) in enumerate(pairs)]
        for load in loads[:4]:
            load.start()
        barrier = pltpu.get_barrier_semaphore()
        for peer in (y_next, y_prev, x_peer, sibling, lo_peer):
            pl.semaphore_signal(barrier, inc=1, device_id=peer, device_id_type=MESH)
        loads[4].start()
        for k in range(1, NZ):
            pl.semaphore_signal(
                barrier, inc=1, device_id=device(y, h, c, lo, lax.rem(z + k, NZ)), device_id_type=MESH
            )

    def place_rows(half, place, count):
        start = (half * NY + place) * (NH * NC * HALF)
        return pl.ds(start, count * NH * NC * HALF)

    def rows_at(place, hh, cc, half):
        start = (((half * NY + place) * NH + hh) * NC + cc) * HALF
        return pl.ds(pl.multiple_of(start, HALF), HALF)

    def copy(rows, send, recv, peer):
        return pltpu.make_async_remote_copy(
            src_ref=cond.at[rows], dst_ref=cond.at[rows], send_sem=send, recv_sem=recv,
            device_id=peer, device_id_type=MESH,
        )

    def stream_rows(stream, place):
        return rows_at(place, 1 - h if stream == 2 else h, c, 0 if stream == 0 else 1)

    def y_copy(stream, up, step):
        src_place = 0 if step == 0 else 2 * step - 1 + up
        index = (step * 3 + stream) * 2 + up
        return pltpu.make_async_remote_copy(
            src_ref=cond.at[stream_rows(stream, src_place)],
            dst_ref=cond.at[stream_rows(stream, 2 * (step + 1) - 1 + up)],
            send_sem=y_send.at[index], recv_sem=y_recv.at[index],
            device_id=y_prev if up else y_next, device_id_type=MESH,
        )

    def y4_copy(stream):
        down = lax.rem(c + stream, 2)
        peer = lax.rem(y + jnp.where(down == 1, NY - 1, 1), NY)
        return pltpu.make_async_remote_copy(
            src_ref=cond.at[stream_rows(stream, 5 + down)], dst_ref=cond.at[stream_rows(stream, 7)],
            send_sem=y4_send.at[stream], recv_sem=y4_recv.at[stream],
            device_id=device(peer, h, c, lo, z), device_id_type=MESH,
        )

    def x_copy(place, own, half=0):
        index = place if half == 0 else NY
        return copy(rows_at(place, h if own else 1 - h, c, half), x_send.at[index], x_recv.at[index], x_peer)

    def s_copy(place, hh_own, half, own):
        hh = h if hh_own else 1 - h
        index = (place * NH + (0 if hh_own else 1)) * 2 + half
        return copy(rows_at(place, hh, c if own else 1 - c, half), s_send.at[index], s_recv.at[index], sibling)

    def z_copy(half, place, hh, zm, blk):
        index = (half * NY + place) * NH + hh
        rows = pl.ds(pl.multiple_of(index * (NC * HALF), NC * HALF), NC * HALF)
        return pltpu.make_async_remote_copy(
            src_ref=outbox.at[rows], dst_ref=inbox.at[blk, half, z],
            send_sem=z_send.at[index], recv_sem=z_recv.at[(blk * 2 + half) * NZ + z],
            device_id=device(y, h, c, lo, zm), device_id_type=MESH,
        )

    def owner(shift, hh):
        m = lax.rem(y + shift, NY) * NH + hh
        return lax.rem(m, NZ), m // NZ

    def send_sums(half, place, places):
        for k in range(places):
            at, shift = place + k, SHIFTS[place + k]
            for hh in range(NH):
                zm, blk = owner(shift, hh)

                @pl.when(zm != z)
                def _():
                    z_copy(half, at, hh, zm, blk).start()

                @pl.when(zm == z)
                def _():
                    start = pl.multiple_of(((half * NY + at) * NH + hh) * (NC * HALF), NC * HALF)
                    inbox[blk, half, z] = outbox[pl.ds(start, NC * HALF), :]

    def multiply(half, place, places):
        for k in range(places):
            for own in (True, False):
                s_copy(place + k, own, half, False).wait_recv()
        rows = place_rows(half, place, places)
        outbox[rows, :] = dot(cond[rows, :], turned_t[...]).astype(BF16)
        send_sums(half, place, places)

    def multiply_both(place, places):
        for half in range(2):
            for k in range(places):
                for own in (True, False):
                    s_copy(place + k, own, half, False).wait_recv()
        count = places * NH * NC * HALF
        rows = [place_rows(half, place, places) for half in range(2)]
        product = dot(jnp.concatenate([cond[r, :] for r in rows], axis=0), turned_t[...]).astype(BF16)
        for half in range(2):
            outbox[rows[half], :] = product[half * count : (half + 1) * count]
        for half in range(2):
            send_sums(half, place, places)

    def arrive(stream, step):
        with jax.named_scope(f"y_{stream}_{step}"):
            for up in range(2):
                y_copy(stream, up, step - 1).wait_recv()
                if step < 3:
                    y_copy(stream, up, step).start()
            if step == 3:
                y4_copy(stream).start()
            for up in range(2):
                place = 2 * step - 1 + up
                if stream == 0:
                    x_copy(place, True).start()
                s_copy(place, stream != 2, 0 if stream == 0 else 1, True).start()

    def arrive_far(stream):
        with jax.named_scope(f"y_{stream}_4"):
            y4_copy(stream).wait_recv()
            if stream == 0:
                x_copy(7, True).start()
            s_copy(7, stream != 2, 0 if stream == 0 else 1, True).start()

    def arrive_x(*places):
        with jax.named_scope(f"x_{places[0]}"):
            for place in places:
                x_copy(place, False).wait_recv()
                s_copy(place, False, 0, True).start()

    def condition(half):
        pieces = precondition(q_ref[half * HALF : (half + 1) * HALF, :], mats, rows_ref, turned_ref)
        for p, piece in enumerate(pieces):
            cond[rows_at(0, h, c, half), p * LANES : (p + 1) * LANES] = piece

    with jax.named_scope("load"):
        for load in loads[:4]:
            load.wait()
    with jax.named_scope("condition_0"):
        mats = weights(bi_ref, bo_ref, eig_ref)
        condition(0)
    with jax.named_scope("barrier"):
        pl.semaphore_wait(barrier, 12)
    y_copy(0, 0, 0).start()
    y_copy(0, 1, 0).start()
    with jax.named_scope("condition_1"):
        condition(1)
    x_copy(0, True, 1).start()
    y_copy(1, 0, 0).start()
    y_copy(1, 1, 0).start()
    x_copy(0, True).start()
    s_copy(0, True, 0, True).start()
    s_copy(0, True, 1, True).start()
    arrive(0, 1)
    with jax.named_scope("x_other"):
        x_copy(0, False, 1).wait_recv()
    y_copy(2, 0, 0).start()
    y_copy(2, 1, 0).start()
    with jax.named_scope("turn_train"):
        loads[4].wait()

        def turn_train(k, _):
            part = pl.ds(pl.multiple_of(k * TURN, TURN), TURN)
            turned_t[part, :] = t_ref[:, part].T
            return 0

        lax.fori_loop(0, GRAD // TURN, turn_train, 0)
    s_copy(0, False, 1, True).start()
    arrive_x(0)
    multiply_both(0, 1)
    arrive(0, 2)
    arrive(1, 1)
    arrive(2, 1)
    arrive_x(1, 2)
    multiply_both(1, 2)
    arrive(0, 3)
    arrive(1, 2)
    arrive_x(3, 4)
    multiply(0, 3, 2)
    arrive_far(0)
    arrive(2, 2)
    multiply(1, 3, 2)
    arrive_x(5, 6)
    arrive(1, 3)
    multiply(0, 5, 2)
    arrive(2, 3)
    arrive_x(7)
    multiply(0, 7, 1)
    multiply(1, 5, 2)
    arrive_far(1)
    arrive_far(2)
    multiply(1, 7, 1)

    with jax.named_scope("drain"):
        for stream in range(3):
            for step in range(3):
                for up in range(2):
                    y_copy(stream, up, step).wait_send()
            y4_copy(stream).wait_send()
        for place in range(NY):
            x_copy(place, True).wait_send()
            for hh_own in (True, False):
                for half in range(2):
                    s_copy(place, hh_own, half, True).wait_send()
        x_copy(0, True, 1).wait_send()

    def collect(blk, half):
        def await_one(k, _):
            frm = lax.rem(z + k, NZ)
            pltpu.make_async_remote_copy(
                src_ref=inbox.at[blk, half, frm], dst_ref=inbox.at[blk, half, frm],
                send_sem=z_send.at[0], recv_sem=z_recv.at[(blk * 2 + half) * NZ + frm],
                device_id=device(y, h, c, lo, frm), device_id_type=MESH,
            ).wait_recv()
            return 0

        lax.fori_loop(1, NZ, await_one, 0)
        total = inbox[blk, half, 0].astype(F32)
        for k in range(1, NZ):
            total += inbox[blk, half, k].astype(F32)
        return total

    def l_copy(half):
        return pltpu.make_async_remote_copy(
            src_ref=sums.at[half], dst_ref=xbox.at[half], send_sem=l_send.at[half], recv_sem=l_recv.at[half],
            device_id=lo_peer, device_id_type=MESH,
        )

    def drain_sums(half):
        for place in range(NY):
            for hh in range(NH):
                zm, blk = owner(SHIFTS[place], hh)

                @pl.when(zm != z)
                def _():
                    z_copy(half, place, hh, zm, blk).wait_send()

    mine = []
    for half in range(2):
        with jax.named_scope("collect_other"):
            sums[half] = collect(1 - lo, half)
            l_copy(half).start()
        with jax.named_scope("drain_z"):
            drain_sums(half)
        with jax.named_scope("collect_own"):
            mine.append(collect(lo, half))
    with jax.named_scope("finish"):
        for half in range(2):
            l_copy(half).wait_recv()
            total = mine[half] + xbox[half]
            for cc in range(NC):
                out_ref[(cc * 2 + half) * HALF : (cc * 2 + half + 1) * HALF, :] = total[cc * HALF : (cc + 1) * HALF]
    with jax.named_scope("drain_sums"):
        for half in range(2):
            l_copy(half).wait_send()


def per_device(queries, train_grads, basis_in, basis_out, inverse_eigen):
    hbm = pl.BlockSpec(memory_space=pl.ANY)
    vmem = pl.BlockSpec(memory_space=pltpu.VMEM)
    dma = pltpu.SemaphoreType.DMA
    return pl.pallas_call(
        kernel,
        out_shape=jax.ShapeDtypeStruct((BLOCK, COLS), F32),
        in_specs=[hbm] * 5,
        out_specs=vmem,
        scratch_shapes=[
            pltpu.VMEM((2 * HALF, GRAD), BF16),
            pltpu.VMEM((COLS, GRAD), BF16),
            pltpu.VMEM((GRAD, COLS), BF16),
            pltpu.VMEM((WIDTH, WIDTH), F32),
            pltpu.VMEM((WIDTH, WIDTH), F32),
            pltpu.VMEM((WIDTH, WIDTH), F32),
            pltpu.VMEM((NY * NH * BLOCK, GRAD), BF16),
            pltpu.VMEM((NY * NH * BLOCK, COLS), BF16),
            pltpu.VMEM((NL, 2, NZ, NC * HALF, COLS), BF16),
            pltpu.VMEM((2, NC * HALF, COLS), F32),
            pltpu.VMEM((2, NC * HALF, COLS), F32),
            pltpu.VMEM((PAIRS * HALF, LANES), F32),
            pltpu.VMEM((PAIRS * HALF, LANES), F32),
            dma((5,)),
            dma((18,)), dma((18,)),
            dma((3,)), dma((3,)),
            dma((9,)), dma((9,)),
            dma((32,)), dma((32,)),
            dma((32,)), dma((32,)),
            dma((2,)), dma((2,)),
        ],
        compiler_params=pltpu.CompilerParams(
            collective_id=0, has_side_effects=True, vmem_limit_bytes=60 * 1024 * 1024
        ),
        cost_estimate=pl.CostEstimate(
            flops=2 * 1024 * GRAD * COLS, bytes_accessed=5 * 1024 * 1024, transcendentals=0
        ),
        name="influence",
    )(queries, train_grads, basis_in, basis_out, inverse_eigen)


def solution(mesh):
    in_specs = (
        P("layer", "ex", None),
        P("layer", "ex", None),
        P("layer", None, None),
        P("layer", None, None),
        P("layer", None, None),
    )
    out_specs = P("layer", "ex")
    return jax.shard_map(
        per_device, mesh=mesh, in_specs=in_specs, out_specs=out_specs, check_vma=False
    )
```

```python
import functools

import jax
import jax.numpy as jnp
from jax import lax
from jax.experimental import pallas as pl
from jax.experimental.pallas import tpu as pltpu
from jax.sharding import PartitionSpec as P

MESH = pl.DeviceIdType.MESH
NY, NH, NC = 8, 2, 2
NL, NZ = 2, 8
HALF = 16
WIDTH = 64
GRAD = WIDTH * WIDTH
LANES = 128
PAIRS = GRAD // LANES
BLOCK = 64
COLS = 512
TURN = 256
SHIFTS = (0, 7, 1, 6, 2, 5, 3, 4)
F32, BF16 = jnp.float32, jnp.bfloat16


def split(value):
    high = value.astype(BF16)
    return high, (value - high.astype(F32)).astype(BF16)


def dot(left, right, dims=((1,), (0,))):
    return lax.dot_general(left, right, (dims, ((), ())), preferred_element_type=F32)


def twice(value):
    return jnp.concatenate([value, value], axis=1)


def lower_half(shape):
    return lax.rem(lax.broadcasted_iota(jnp.int32, shape, 1), LANES) < WIDTH


def weights(bi_ref, bo_ref, eig_ref):
    wide = twice(bi_ref[...])
    low = lower_half(wide.shape)
    diag = jnp.concatenate([jnp.where(low, wide, 0.0), jnp.where(low, 0.0, wide)], axis=0)
    diag_hi, diag_lo = split(diag)
    first = jnp.concatenate([diag_hi, diag_lo], axis=0)
    last = jnp.concatenate([diag_hi, diag_hi, diag_lo], axis=1)
    even, odd = bo_ref[pl.ds(0, PAIRS, stride=2), :], bo_ref[pl.ds(1, PAIRS, stride=2), :]
    rows = jnp.concatenate([even, odd], axis=1)
    rows_hi = rows.astype(BF16).astype(F32)
    rows_lo = rows - rows_hi
    into = jnp.transpose(jnp.concatenate([rows_hi, rows_hi, rows_lo, rows_lo], axis=0)).astype(BF16)
    stack = jnp.concatenate([even, odd], axis=0)
    stack_hi = stack.astype(BF16).astype(F32)
    back = jnp.concatenate([twice(stack_hi), twice(stack - stack_hi)], axis=1).astype(BF16)
    return first, into, twice(eig_ref[...]), back, last


def precondition(block, mats, rows_ref, turned_ref):
    first, into, eig, back, last = mats
    stacked = jnp.concatenate([block[:, p * LANES : (p + 1) * LANES] for p in range(PAIRS)], axis=0)
    rows_ref[...] = dot(jnp.concatenate([stacked, stacked], axis=1), first)
    right = jnp.concatenate([rows_ref[pl.ds(q, PAIRS, stride=HALF), :] for q in range(HALF)], axis=1)
    right_hi, right_lo = split(right)
    both = dot(into, jnp.concatenate([right_hi, right_lo, right_hi, right_lo], axis=0))
    low = lower_half((WIDTH, HALF * LANES))
    picked = jnp.where(low, both[:WIDTH], both[WIDTH:])
    scaled = []
    for q in range(HALF):
        part = picked[:, q * LANES : (q + 1) * LANES]
        scaled.append((part + pltpu.roll(part, WIDTH, 1)) * eig)
    scaled_hi, scaled_lo = split(jnp.concatenate(scaled, axis=1))
    left = dot(back, jnp.concatenate([scaled_hi, scaled_lo, scaled_hi, scaled_lo], axis=0))
    left = jnp.where(lower_half((PAIRS, HALF * LANES)), left[:PAIRS], left[PAIRS:])
    left = jnp.concatenate([left[:, q * LANES : (q + 1) * LANES] for q in range(HALF)], axis=0)
    left_hi, left_lo = split(left)
    full = dot(jnp.concatenate([left_hi, left_lo, left_hi], axis=1), last, ((1,), (1,)))
    for q in range(HALF):
        turned_ref[pl.ds(q, PAIRS, stride=HALF), :] = full[q * PAIRS : (q + 1) * PAIRS]
    return [turned_ref[p * HALF : (p + 1) * HALF, :].astype(BF16) for p in range(PAIRS)]


def kernel(
    q_hbm, t_hbm, bi_hbm, bo_hbm, eig_hbm, out_ref,
    q_ref, t_ref, turned_t, bi_ref, bo_ref, eig_ref, cond, outbox, inbox, xbox, sums, rows_ref, turned_ref,
    load_sem, y_send, y_recv, y4_send, y4_recv, x_send, x_recv, s_send, s_recv, z_send, z_recv, l_send, l_recv,
):
    ex, layer = lax.axis_index("ex"), lax.axis_index("layer")
    y, h, c = ex // (NH * NC), lax.rem(ex // NC, NH), lax.rem(ex, NC)
    lo, z = layer // NZ, lax.rem(layer, NZ)

    def device(yy, hh, cc, ll, zz):
        return ((yy * NH + hh) * NC + cc, ll * NZ + zz)

    y_next = device(lax.rem(y + 1, NY), h, c, lo, z)
    y_prev = device(lax.rem(y + NY - 1, NY), h, c, lo, z)
    x_peer = device(y, 1 - h, c, lo, z)
    sibling = device(y, h, 1 - c, lo, z)
    lo_peer = device(y, h, c, 1 - lo, z)

    with jax.named_scope("greet"):
        pairs = [(q_hbm, q_ref), (bi_hbm, bi_ref), (bo_hbm, bo_ref), (eig_hbm, eig_ref), (t_hbm, t_ref)]
        loads = [pltpu.make_async_copy(src.at[0], dst, load_sem.at[i]) for i, (src, dst) in enumerate(pairs)]
        for load in loads[:4]:
            load.start()
        barrier = pltpu.get_barrier_semaphore()
        for peer in (y_next, y_prev, x_peer, sibling, lo_peer):
            pl.semaphore_signal(barrier, inc=1, device_id=peer, device_id_type=MESH)
        loads[4].start()
        for k in range(1, NZ):
            pl.semaphore_signal(
                barrier, inc=1, device_id=device(y, h, c, lo, lax.rem(z + k, NZ)), device_id_type=MESH
            )

    def place_rows(half, place, count):
        start = (half * NY + place) * (NH * NC * HALF)
        return pl.ds(start, count * NH * NC * HALF)

    def rows_at(place, hh, cc, half):
        start = (((half * NY + place) * NH + hh) * NC + cc) * HALF
        return pl.ds(pl.multiple_of(start, HALF), HALF)

    def copy(rows, send, recv, peer):
        return pltpu.make_async_remote_copy(
            src_ref=cond.at[rows], dst_ref=cond.at[rows], send_sem=send, recv_sem=recv,
            device_id=peer, device_id_type=MESH,
        )

    def stream_rows(stream, place):
        return rows_at(place, 1 - h if stream == 2 else h, c, 0 if stream == 0 else 1)

    def y_copy(stream, up, step):
        src_place = 0 if step == 0 else 2 * step - 1 + up
        index = (step * 3 + stream) * 2 + up
        return pltpu.make_async_remote_copy(
            src_ref=cond.at[stream_rows(stream, src_place)],
            dst_ref=cond.at[stream_rows(stream, 2 * (step + 1) - 1 + up)],
            send_sem=y_send.at[index], recv_sem=y_recv.at[index],
            device_id=y_prev if up else y_next, device_id_type=MESH,
        )

    def y4_copy(stream):
        down = lax.rem(c + stream, 2)
        peer = lax.rem(y + jnp.where(down == 1, NY - 1, 1), NY)
        return pltpu.make_async_remote_copy(
            src_ref=cond.at[stream_rows(stream, 5 + down)], dst_ref=cond.at[stream_rows(stream, 7)],
            send_sem=y4_send.at[stream], recv_sem=y4_recv.at[stream],
            device_id=device(peer, h, c, lo, z), device_id_type=MESH,
        )

    def x_copy(place, own, half=0):
        index = place if half == 0 else NY
        return copy(rows_at(place, h if own else 1 - h, c, half), x_send.at[index], x_recv.at[index], x_peer)

    def s_copy(place, hh_own, half, own):
        hh = h if hh_own else 1 - h
        index = (place * NH + (0 if hh_own else 1)) * 2 + half
        return copy(rows_at(place, hh, c if own else 1 - c, half), s_send.at[index], s_recv.at[index], sibling)

    def z_copy(half, place, hh, zm, blk):
        index = (half * NY + place) * NH + hh
        rows = pl.ds(pl.multiple_of(index * (NC * HALF), NC * HALF), NC * HALF)
        return pltpu.make_async_remote_copy(
            src_ref=outbox.at[rows], dst_ref=inbox.at[blk, half, z],
            send_sem=z_send.at[index], recv_sem=z_recv.at[(blk * 2 + half) * NZ + z],
            device_id=device(y, h, c, lo, zm), device_id_type=MESH,
        )

    def owner(shift, hh):
        m = lax.rem(y + shift, NY) * NH + hh
        return lax.rem(m, NZ), m // NZ

    def send_sums(half, place, places):
        for k in range(places):
            at, shift = place + k, SHIFTS[place + k]
            for hh in range(NH):
                zm, blk = owner(shift, hh)

                @pl.when(zm != z)
                def _():
                    z_copy(half, at, hh, zm, blk).start()

                @pl.when(zm == z)
                def _():
                    start = pl.multiple_of(((half * NY + at) * NH + hh) * (NC * HALF), NC * HALF)
                    inbox[blk, half, z] = outbox[pl.ds(start, NC * HALF), :]

    def multiply(half, place, places):
        for k in range(places):
            for own in (True, False):
                s_copy(place + k, own, half, False).wait_recv()
        rows = place_rows(half, place, places)
        outbox[rows, :] = dot(cond[rows, :], turned_t[...]).astype(BF16)
        send_sums(half, place, places)

    def multiply_both(place, places):
        for half in range(2):
            for k in range(places):
                for own in (True, False):
                    s_copy(place + k, own, half, False).wait_recv()
        count = places * NH * NC * HALF
        rows = [place_rows(half, place, places) for half in range(2)]
        product = dot(jnp.concatenate([cond[r, :] for r in rows], axis=0), turned_t[...]).astype(BF16)
        for half in range(2):
            outbox[rows[half], :] = product[half * count : (half + 1) * count]
        for half in range(2):
            send_sums(half, place, places)

    def arrive(stream, step):
        with jax.named_scope(f"y_{stream}_{step}"):
            for up in range(2):
                y_copy(stream, up, step - 1).wait_recv()
                if step < 3:
                    y_copy(stream, up, step).start()
            if step == 3:
                y4_copy(stream).start()
            for up in range(2):
                place = 2 * step - 1 + up
                if stream == 0:
                    x_copy(place, True).start()
                s_copy(place, stream != 2, 0 if stream == 0 else 1, True).start()

    def arrive_far(stream):
        with jax.named_scope(f"y_{stream}_4"):
            y4_copy(stream).wait_recv()
            if stream == 0:
                x_copy(7, True).start()
            s_copy(7, stream != 2, 0 if stream == 0 else 1, True).start()

    def arrive_x(*places):
        with jax.named_scope(f"x_{places[0]}"):
            for place in places:
                x_copy(place, False).wait_recv()
                s_copy(place, False, 0, True).start()

    def condition(half):
        pieces = precondition(q_ref[half * HALF : (half + 1) * HALF, :], mats, rows_ref, turned_ref)
        for p, piece in enumerate(pieces):
            cond[rows_at(0, h, c, half), p * LANES : (p + 1) * LANES] = piece

    with jax.named_scope("load"):
        for load in loads[:4]:
            load.wait()
    with jax.named_scope("condition_0"):
        mats = weights(bi_ref, bo_ref, eig_ref)
        condition(0)
    with jax.named_scope("barrier"):
        pl.semaphore_wait(barrier, 12)
    y_copy(0, 0, 0).start()
    y_copy(0, 1, 0).start()
    with jax.named_scope("condition_1"):
        condition(1)
    x_copy(0, True, 1).start()
    y_copy(1, 0, 0).start()
    y_copy(1, 1, 0).start()
    x_copy(0, True).start()
    s_copy(0, True, 0, True).start()
    s_copy(0, True, 1, True).start()
    arrive(0, 1)
    with jax.named_scope("x_other"):
        x_copy(0, False, 1).wait_recv()
    y_copy(2, 0, 0).start()
    y_copy(2, 1, 0).start()
    with jax.named_scope("turn_train"):
        loads[4].wait()

        def turn_train(k, _):
            part = pl.ds(pl.multiple_of(k * TURN, TURN), TURN)
            turned_t[part, :] = t_ref[:, part].T
            return 0

        lax.fori_loop(0, GRAD // TURN, turn_train, 0)
    s_copy(0, False, 1, True).start()
    arrive_x(0)
    arrive(0, 2)
    arrive(1, 1)
    multiply_both(0, 1)
    arrive(2, 1)
    arrive_x(1, 2)
    multiply_both(1, 2)
    arrive(0, 3)
    arrive(1, 2)
    arrive_x(3, 4)
    multiply(0, 3, 2)
    arrive_far(0)
    arrive(2, 2)
    multiply(1, 3, 2)
    arrive_x(5, 6)
    arrive(1, 3)
    multiply(0, 5, 2)
    arrive(2, 3)
    arrive_x(7)
    multiply(0, 7, 1)
    multiply(1, 5, 2)
    arrive_far(1)
    arrive_far(2)
    multiply(1, 7, 1)

    with jax.named_scope("drain"):
        for stream in range(3):
            for step in range(3):
                for up in range(2):
                    y_copy(stream, up, step).wait_send()
            y4_copy(stream).wait_send()
        for place in range(NY):
            x_copy(place, True).wait_send()
            for hh_own in (True, False):
                for half in range(2):
                    s_copy(place, hh_own, half, True).wait_send()
        x_copy(0, True, 1).wait_send()

    def collect(blk, half):
        def await_one(k, _):
            frm = lax.rem(z + k, NZ)
            pltpu.make_async_remote_copy(
                src_ref=inbox.at[blk, half, frm], dst_ref=inbox.at[blk, half, frm],
                send_sem=z_send.at[0], recv_sem=z_recv.at[(blk * 2 + half) * NZ + frm],
                device_id=device(y, h, c, lo, frm), device_id_type=MESH,
            ).wait_recv()
            return 0

        lax.fori_loop(1, NZ, await_one, 0)
        total = inbox[blk, half, 0].astype(F32)
        for k in range(1, NZ):
            total += inbox[blk, half, k].astype(F32)
        return total

    def l_copy(half):
        return pltpu.make_async_remote_copy(
            src_ref=sums.at[half], dst_ref=xbox.at[half], send_sem=l_send.at[half], recv_sem=l_recv.at[half],
            device_id=lo_peer, device_id_type=MESH,
        )

    def drain_sums(half):
        for place in range(NY):
            for hh in range(NH):
                zm, blk = owner(SHIFTS[place], hh)

                @pl.when(zm != z)
                def _():
                    z_copy(half, place, hh, zm, blk).wait_send()

    mine = []
    for half in range(2):
        with jax.named_scope("collect_other"):
            sums[half] = collect(1 - lo, half)
            l_copy(half).start()
        with jax.named_scope("drain_z"):
            drain_sums(half)
        with jax.named_scope("collect_own"):
            mine.append(collect(lo, half))
    with jax.named_scope("finish"):
        for half in range(2):
            l_copy(half).wait_recv()
            total = mine[half] + xbox[half]
            for cc in range(NC):
                out_ref[(cc * 2 + half) * HALF : (cc * 2 + half + 1) * HALF, :] = total[cc * HALF : (cc + 1) * HALF]
    with jax.named_scope("drain_sums"):
        for half in range(2):
            l_copy(half).wait_send()


def per_device(queries, train_grads, basis_in, basis_out, inverse_eigen):
    hbm = pl.BlockSpec(memory_space=pl.ANY)
    vmem = pl.BlockSpec(memory_space=pltpu.VMEM)
    dma = pltpu.SemaphoreType.DMA
    return pl.pallas_call(
        kernel,
        out_shape=jax.ShapeDtypeStruct((BLOCK, COLS), F32),
        in_specs=[hbm] * 5,
        out_specs=vmem,
        scratch_shapes=[
            pltpu.VMEM((2 * HALF, GRAD), BF16),
            pltpu.VMEM((COLS, GRAD), BF16),
            pltpu.VMEM((GRAD, COLS), BF16),
            pltpu.VMEM((WIDTH, WIDTH), F32),
            pltpu.VMEM((WIDTH, WIDTH), F32),
            pltpu.VMEM((WIDTH, WIDTH), F32),
            pltpu.VMEM((NY * NH * BLOCK, GRAD), BF16),
            pltpu.VMEM((NY * NH * BLOCK, COLS), BF16),
            pltpu.VMEM((NL, 2, NZ, NC * HALF, COLS), BF16),
            pltpu.VMEM((2, NC * HALF, COLS), F32),
            pltpu.VMEM((2, NC * HALF, COLS), F32),
            pltpu.VMEM((PAIRS * HALF, LANES), F32),
            pltpu.VMEM((PAIRS * HALF, LANES), F32),
            dma((5,)),
            dma((18,)), dma((18,)),
            dma((3,)), dma((3,)),
            dma((9,)), dma((9,)),
            dma((32,)), dma((32,)),
            dma((32,)), dma((32,)),
            dma((2,)), dma((2,)),
        ],
        compiler_params=pltpu.CompilerParams(
            collective_id=0, has_side_effects=True, vmem_limit_bytes=60 * 1024 * 1024
        ),
        cost_estimate=pl.CostEstimate(
            flops=2 * 1024 * GRAD * COLS, bytes_accessed=5 * 1024 * 1024, transcendentals=0
        ),
        name="influence",
    )(queries, train_grads, basis_in, basis_out, inverse_eigen)


def solution(mesh):
    in_specs = (
        P("layer", "ex", None),
        P("layer", "ex", None),
        P("layer", None, None),
        P("layer", None, None),
        P("layer", None, None),
    )
    out_specs = P("layer", "ex")
    return jax.shard_map(
        per_device, mesh=mesh, in_specs=in_specs, out_specs=out_specs, check_vma=False
    )
```
